32 devices in a mesh: batch: 4 (over y, x), seq: 4 (over z), head: 2 (over core).
Axes of the slice: x: 2, y: 2, z: 4, core: 2. Of those that a mesh axis runs over, the one named last changes fastest.
Arguments:
- hidden: bfloat16 [8, 4096, 1024], P('batch', 'seq', 'head'), may hold values from -6 to 6
- cotangent: bfloat16 [8, 4096, 1024], P('batch', 'seq', 'head'), may hold values from -6 to 6
- norm_gain: bfloat16 [1024], P('head'), may hold values from 0.099609375 to 1.8984375
- proj_gate: bfloat16 [1024, 2048], P(None, 'head'), may hold values from -0.1875 to 0.1875
- proj_values: bfloat16 [1024, 2048], P(None, 'head'), may hold values from -0.1875 to 0.1875
- proj_state: bfloat16 [1024, 256], P(None, 'head'), may hold values from -0.1875 to 0.1875
- proj_steps: bfloat16 [1024, 32], P(None, 'head'), may hold values from -0.1875 to 0.1875
- conv_values: float32 [4, 2048], P(None, 'head'), may hold values from -3 to 3
- conv_state: float32 [4, 256], P(None, 'head'), may hold values from -3 to 3
- bias_values: float32 [2048], P('head'), may hold values from -2 to 2
- bias_state: float32 [256], P('head'), may hold values from -2 to 2
- step_bias: float32 [32], P('head'), may hold values from -6 to -1
- log_rates: float32 [32], P('head'), may hold values from -3 to 1
- skip_gain: float32 [32], P('head'), may hold values from 0.5 to 1.5
- gate_gain: float32 [2048], P('head'), may hold values from 0.1 to 1.9
- proj_output: bfloat16 [2048, 1024], P('head'), may hold values from -0.125 to 0.125
Outputs:
- block_out: bfloat16 [8, 4096, 1024], P('batch', 'seq', 'head')
- grad_hidden: float32 [8, 4096, 1024], P('batch', 'seq', 'head')
- grad_norm_gain: float32 [1024], P('head')
- grad_proj_gate: float32 [1024, 2048], P(None, 'head')
- grad_proj_values: float32 [1024, 2048], P(None, 'head')
- grad_proj_state: float32 [1024, 256], P(None, 'head')
- grad_proj_steps: float32 [1024, 32], P(None, 'head')
- grad_conv_values: float32 [4, 2048], P(None, 'head')
- grad_conv_state: float32 [4, 256], P(None, 'head')
- grad_bias_values: float32 [2048], P('head')
- grad_bias_state: float32 [256], P('head')
- grad_step_bias: float32 [32], P('head')
- grad_log_rates: float32 [32], P('head')
- grad_skip_gain: float32 [32], P('head')
- grad_gate_gain: float32 [2048], P('head')
- grad_proj_output: float32 [2048, 1024], P('head')
The draws below stay inside these ranges and needn't reach their ends.
All inputs are finite; a program needn't handle non-finite values.
Results may differ from the reference program's by a relative error of at most 0.0093.
Values may be sent and summed in bfloat16 or wider, within the bound.
A program may use at most 512 MiB of HBM per device.

```python
import jax
import jax.numpy as jnp
from jax import lax

D = 1024
INNER = 2048
HEADDIM = 64
STATE = 128
WIN = 4
SPAN = 256
HEADS = 32
LENGTH = 4096
SEQS = 8


def levels(stream_key, shape, shards, least, largest):
    level = 1.0
    for dim, parts in shards:
        draws = jax.random.uniform(jax.random.fold_in(jax.random.fold_in(stream_key, 6), dim), (parts,), jnp.float32, least / len(shards), largest / len(shards))
        level = level * jnp.repeat(jnp.exp(draws), shape[dim] // parts).reshape((-1,) + (1,) * (len(shape) - 1 - dim))
    return level


def scatter_about(key, shape, scale, most, shards=(), kind=jnp.bfloat16):
    drawn = scale * jax.random.normal(key, shape, jnp.float32)
    if shards:
        drawn = drawn * levels(key, shape, shards, -0.22, 0.18)
    return jnp.clip(drawn, -most, most).astype(kind)


def setup_inputs(seed: int = 0) -> dict:
    key_list = jax.random.split(jax.random.key(seed), 17)
    return {
        "hidden": scatter_about(key_list[0], (SEQS, LENGTH, D), 1.0, 6.0, ((0, 4), (1, 4), (2, 2))),
        "cotangent": scatter_about(key_list[1], (SEQS, LENGTH, D), 1.0, 6.0, ((0, 4), (1, 4), (2, 2))),
        "norm_gain": jnp.clip(1.0 + 0.18 * jax.random.normal(key_list[2], (D,), jnp.float32), 0.099609375, 1.8984375).astype(jnp.bfloat16),
        "proj_gate": scatter_about(key_list[3], (D, INNER), D ** -0.5, 0.1875, ((1, 2),)),
        "proj_values": scatter_about(key_list[4], (D, INNER), D ** -0.5, 0.1875, ((1, 2),)),
        "proj_state": scatter_about(key_list[5], (D, 2 * STATE), D ** -0.5, 0.1875, ((1, 2),)),
        "proj_steps": scatter_about(key_list[6], (D, HEADS), D ** -0.5, 0.1875, ((1, 2),)),
        "conv_values": scatter_about(key_list[7], (WIN, INNER), WIN ** -0.5, 3.0, ((1, 2),), jnp.float32),
        "conv_state": scatter_about(key_list[8], (WIN, 2 * STATE), WIN ** -0.5, 3.0, ((1, 2),), jnp.float32),
        "bias_values": scatter_about(key_list[9], (INNER,), 0.3, 2.0, ((0, 2),), jnp.float32),
        "bias_state": scatter_about(key_list[10], (2 * STATE,), 0.3, 2.0, ((0, 2),), jnp.float32),
        "step_bias": jnp.clip(-6.0 + 5.0 * jax.random.uniform(key_list[11], (HEADS,), jnp.float32) ** levels(key_list[11], (HEADS,), ((0, 2),), -0.2, 0.2), -6.0, -1.0),
        "log_rates": jnp.clip(-3.0 + 4.0 * jax.random.uniform(key_list[12], (HEADS,), jnp.float32) ** levels(key_list[12], (HEADS,), ((0, 2),), -0.2, 0.2), -3.0, 1.0),
        "skip_gain": jnp.clip(0.5 + 1.0 * jax.random.uniform(key_list[13], (HEADS,), jnp.float32) ** levels(key_list[13], (HEADS,), ((0, 2),), -0.2, 0.2), 0.5, 1.5),
        "gate_gain": jnp.clip(1.0 + 0.18 * jax.random.normal(key_list[14], (INNER,), jnp.float32), 0.1, 1.9),
        "proj_output": scatter_about(key_list[15], (INNER, D), INNER ** -0.5, 0.125, ((0, 2),)),
    }


@jax.custom_vjp
def low(v):
    return lax.optimization_barrier(v.astype(jnp.bfloat16)).astype(jnp.float32)

@jax.custom_vjp
def low_back(v):
    return v

def low_keep(v):
    return (low(v), None)

def low_pass(kept, grad):
    return (grad,)

def back_keep(v):
    return (v, None)

def back_low(kept, grad):
    return (low(grad),)
low.defvjp(low_keep, low_pass)
low_back.defvjp(back_keep, back_low)
epsilon = 1e-05
highest = lax.Precision.HIGHEST

def ssd_sequence(values, steps, rates, writes, readout):
    length = steps.shape[0]
    blocks = length // SPAN
    causal = jnp.tril(jnp.ones((SPAN, SPAN), dtype=bool))

    def span_step(state, block):
        block_values, block_steps, block_writes, block_reads = block
        cumul = jnp.cumsum(block_steps * rates, axis=0)
        scores = jnp.dot(block_reads, block_writes.T, precision=highest)
        differ = cumul[:, None, :] - cumul[None, :, :]
        decays = jnp.where(causal[:, :, None], jnp.exp(jnp.where(causal[:, :, None], differ, 0.0)), 0.0)
        mixing = decays * scores[:, :, None] * block_steps[None, :, :]
        inner = jnp.einsum('tuh,uhp->thp', mixing, block_values, precision=highest)
        carried = jnp.einsum('tn,hpn->thp', block_reads, state, precision=highest) * jnp.exp(cumul)[:, :, None]
        total = cumul[-1]
        tail = jnp.exp(total[None, :] - cumul) * block_steps
        fresh = jnp.einsum('uh,uhp,un->hpn', tail, block_values, block_writes, precision=highest)
        return (state * jnp.exp(total)[:, None, None] + fresh, inner + carried)
    start = jnp.zeros((HEADS, HEADDIM, STATE), dtype=jnp.float32)
    blocked = (values.reshape(blocks, SPAN, HEADS, HEADDIM), steps.reshape(blocks, SPAN, HEADS), writes.reshape(blocks, SPAN, STATE), readout.reshape(blocks, SPAN, STATE))
    final_state, outputs = lax.scan(jax.checkpoint(span_step), start, blocked)
    return outputs.reshape(length, HEADS, HEADDIM)

def layer(inputs, norm_gain, proj_gate, proj_values, proj_state, proj_steps, conv_values, conv_state, bias_values, bias_state, step_bias, log_rates, skip_gain, gate_gain, proj_output):
    kernel = jnp.concatenate([conv_values, conv_state], axis=1)
    offset = jnp.concatenate([bias_values, bias_state])

    def one_sequence(rows):
        length = rows.shape[0]
        inv_rms = lax.rsqrt(lax.optimization_barrier(jnp.mean(rows * rows, axis=1, keepdims=True)) + epsilon)
        normed = low(rows * inv_rms * norm_gain)
        gate_pre = low_back(jnp.dot(normed, proj_gate, precision=highest))
        value_pre = low_back(jnp.dot(normed, proj_values, precision=highest))
        state_pre = low_back(jnp.dot(normed, proj_state, precision=highest))
        steps_pre = low_back(jnp.dot(normed, proj_steps, precision=highest))
        mixed_pre = jnp.concatenate([value_pre, state_pre], axis=1)
        padded = jnp.pad(mixed_pre, ((WIN - 1, 0), (0, 0)))
        conv_pre = offset + kernel[0] * padded[0:length]
        for position in range(1, WIN):
            conv_pre = conv_pre + kernel[position] * padded[position:position + length]
        activated = jax.nn.silu(conv_pre)
        values = activated[:, :INNER].reshape(length, HEADS, HEADDIM)
        writes = activated[:, INNER:INNER + STATE]
        readout = activated[:, INNER + STATE:]
        steps = jax.nn.softplus(steps_pre + step_bias)
        rates = -jnp.exp(log_rates)
        core = ssd_sequence(values, steps, rates, writes, readout) + skip_gain[None, :, None] * values
        gated = core.reshape(length, INNER) * jax.nn.silu(gate_pre)
        inv_gate = lax.rsqrt(lax.optimization_barrier(jnp.mean(gated * gated, axis=1, keepdims=True)) + epsilon)
        gate_normed = low(gated * inv_gate * gate_gain)
        return rows + jnp.dot(gate_normed, proj_output, precision=highest)
    return lax.map(jax.checkpoint(one_sequence), inputs)

def reference(hidden, cotangent, norm_gain, proj_gate, proj_values, proj_state, proj_steps, conv_values, conv_state, bias_values, bias_state, step_bias, log_rates, skip_gain, gate_gain, proj_output):
    result, pullback = jax.vjp(layer, hidden.astype(jnp.float32), norm_gain.astype(jnp.float32), proj_gate.astype(jnp.float32), proj_values.astype(jnp.float32), proj_state.astype(jnp.float32), proj_steps.astype(jnp.float32), conv_values, conv_state, bias_values, bias_state, step_bias, log_rates, skip_gain, gate_gain, proj_output.astype(jnp.float32))
    grad_hidden, grad_norm_gain, grad_proj_gate, grad_proj_values, grad_proj_state, grad_proj_steps, grad_conv_values, grad_conv_state, grad_bias_values, grad_bias_state, grad_step_bias, grad_log_rates, grad_skip_gain, grad_gate_gain, grad_proj_output = pullback(cotangent.astype(jnp.float32))
    return (result.astype(jnp.bfloat16), grad_hidden, grad_norm_gain, grad_proj_gate, grad_proj_values, grad_proj_state, grad_proj_steps, grad_conv_values, grad_conv_state, grad_bias_values, grad_bias_state, grad_step_bias, grad_log_rates, grad_skip_gain, grad_gate_gain, grad_proj_output)
```

```python
import functools

import jax
import jax.numpy as jnp
from jax import lax
from jax.experimental import pallas as pl
from jax.experimental.pallas import tpu as pltpu
from jax.sharding import PartitionSpec as P

CHUNK = 128
LANES = 128
epsilon = 1e-05
highest = lax.Precision.HIGHEST
f32 = jnp.float32
bf16 = jnp.bfloat16


def mm(a, b, dims=((1,), (0,))):
    return lax.dot_general(a, b, (dims, ((), ())), preferred_element_type=f32)


def split_mm(a, b):
    high = a.astype(bf16)
    low = (a - high.astype(f32)).astype(bf16)
    return mm(high, b) + mm(low, b)


def pair_decays(cum_ref, cumt_ref, j, causal):
    parts = []
    for h in (2 * j, 2 * j + 1):
        differ = cum_ref[0, :, h : h + 1] - cumt_ref[0, h : h + 1, :]
        parts.append(jnp.exp(jnp.where(causal, differ, -1e30)))
    return parts


def spread(column_ref, j, first):
    return jnp.where(
        first, column_ref[0, :, 2 * j : 2 * j + 1], column_ref[0, :, 2 * j + 1 : 2 * j + 2]
    )


def causal_mask():
    rows = lax.broadcasted_iota(jnp.int32, (CHUNK, CHUNK), 0)
    columns = lax.broadcasted_iota(jnp.int32, (CHUNK, CHUNK), 1)
    return rows >= columns


def forward_kernel(x_ref, st_ref, cum_ref, cumt_ref, b_ref, c_ref, skip_ref, enter_ref,
                   core_ref, states_ref, state):
    pairs = x_ref.shape[2] // LANES

    @pl.when(pl.program_id(1) == 0)
    def _():
        state[...] = enter_ref[0]

    causal = causal_mask()
    first = lax.broadcasted_iota(jnp.int32, (CHUNK, LANES), 1) < LANES // 2
    first_row = lax.broadcasted_iota(jnp.int32, (LANES, LANES), 0) < LANES // 2
    writes, reads = b_ref[0], c_ref[0]
    scores = mm(reads, writes, ((1,), (1,)))
    for j in range(pairs):
        at = slice(j * LANES, (j + 1) * LANES)
        x = x_ref[0, :, at]
        scaled = (x * spread(st_ref, j, first)).astype(bf16)
        zero = jnp.zeros_like(scaled)
        left, right = pair_decays(cum_ref, cumt_ref, j, causal)
        mixing = jnp.concatenate(
            [(left * scores).astype(bf16), (right * scores).astype(bf16)], axis=1
        )
        stacked = jnp.concatenate(
            [jnp.where(first, scaled, zero), jnp.where(first, zero, scaled)], axis=0
        )
        cum = spread(cum_ref, j, first)
        last = cum[CHUNK - 1 :, :]
        entered = state[at, :].astype(bf16)
        states_ref[0, 0, at, :] = entered
        carried = mm(reads, entered, ((1,), (1,))) * jnp.exp(cum)
        core_ref[0, :, at] = mm(mixing, stacked) + carried + skip_ref[:, at] * x
        weighted = (scaled.astype(f32) * jnp.exp(last - cum)).astype(bf16)
        fresh = mm(weighted, writes, ((0,), (0,)))
        end = CHUNK - 1
        decay = jnp.exp(
            jnp.where(
                first_row,
                cum_ref[0, end:, 2 * j : 2 * j + 1],
                cum_ref[0, end:, 2 * j + 1 : 2 * j + 2],
            )
        )
        state[at, :] = state[at, :] * decay + fresh


def backward_kernel(x_ref, dy_ref, core_ref, st_ref, cum_ref, cumt_ref, b_ref, c_ref, skip_ref,
                    states_ref, later_ref, pick_ref,
                    dx_ref, maps_ref, direct_ref, decay_ref,
                    state, state_low, grown, shrunk, balance, product):
    pairs = x_ref.shape[2] // LANES

    @pl.when(pl.program_id(1) == 0)
    def _():
        state[...] = later_ref[0]

    causal = causal_mask()
    first = lax.broadcasted_iota(jnp.int32, (CHUNK, LANES), 1) < LANES // 2
    first_row = lax.broadcasted_iota(jnp.int32, (LANES, LANES), 0) < LANES // 2
    end = CHUNK - 1
    at_end = lax.broadcasted_iota(jnp.int32, (CHUNK, LANES), 0) == end
    writes, reads = b_ref[0], c_ref[0]
    scores = mm(reads, writes, ((1,), (1,)))
    ones = jnp.ones((8, LANES), bf16)
    score_grad = jnp.zeros((CHUNK, CHUNK), f32)
    for j in range(pairs):
        at = slice(j * LANES, (j + 1) * LANES)
        x = x_ref[0, :, at]
        dy = dy_ref[0, :, at]
        step = spread(st_ref, j, first)
        scaled = (x * step).astype(bf16)
        low = dy.astype(bf16)
        zero = jnp.zeros_like(low)
        left, right = pair_decays(cum_ref, cumt_ref, j, causal)
        split = jnp.concatenate(
            [jnp.where(first, low, zero), jnp.where(first, zero, low)], axis=0
        )
        mixing = jnp.concatenate(
            [(left * scores).astype(bf16), (right * scores).astype(bf16)], axis=0
        )
        mixing_grad = mm(split, scaled, ((1,), (1,)))
        score_grad = score_grad + mixing_grad[:CHUNK] * left + mixing_grad[CHUNK:] * right
        cum = spread(cum_ref, j, first)
        last = cum[end:, :]
        grow = jnp.exp(cum)
        shrink = jnp.exp(last - cum)
        later = state[at, :]
        later_low = later.astype(bf16)
        state_low[at, :] = later_low
        through = mm(writes, later_low, ((1,), (1,))) * shrink
        scaled_grad = mm(mixing, split, ((0,), (0,))) + through
        skip = skip_ref[:, at]
        dx_ref[0, :, at] = step * scaled_grad + skip * dy
        kept = scaled.astype(f32)
        entered = states_ref[0, 0, at, :]
        meet = mm(ones, (later * entered.astype(f32)).astype(bf16), ((1,), (1,)))[0:1, :]
        finish = jnp.sum(kept * through, axis=0, keepdims=True) + jnp.exp(last) * meet
        terms = low.astype(f32) * (core_ref[0, :, at] - skip * x) - kept * scaled_grad
        balance[:, at] = terms + jnp.where(at_end, finish, 0.0)
        product[:, at] = x * scaled_grad
        grown_here = (dy * grow).astype(bf16)
        grown[:, at] = grown_here
        shrunk[:, at] = (kept * shrink).astype(bf16)
        decay = jnp.exp(
            jnp.where(
                first_row,
                cum_ref[0, end:, 2 * j : 2 * j + 1],
                cum_ref[0, end:, 2 * j + 1 : 2 * j + 2],
            )
        )
        state[at, :] = later * decay + mm(grown_here, reads, ((0,), (0,)))
    score_low = score_grad.astype(bf16)
    maps_ref[0, :, LANES:] = mm(score_low, writes) + mm(grown[...], states_ref[0, 0])
    maps_ref[0, :, :LANES] = mm(score_low, reads, ((0,), (0,))) + mm(shrunk[...], state_low[...])
    direct_ref[0] = split_mm(product[...], pick_ref[...])
    sums = split_mm(balance[...], pick_ref[...])
    upper = lax.broadcasted_iota(jnp.int32, (CHUNK, CHUNK), 0) <= lax.broadcasted_iota(
        jnp.int32, (CHUNK, CHUNK), 1
    )
    upper = upper.astype(f32)
    decay_ref[0] = jnp.dot(upper, sums, precision=highest, preferred_element_type=f32)


def whole_block(array):
    return pl.BlockSpec(array.shape, lambda g, c: (0,) * array.ndim)


def run_forward(values, steps, cum, cumt, writes, reads, skip, entering):
    groups, length, inner = values.shape
    heads, size = steps.shape[2], writes.shape[2]
    chunks = length // CHUNK

    def rows(width):
        return pl.BlockSpec((1, CHUNK, width), lambda g, c: (g, c, 0))

    return pl.pallas_call(
        forward_kernel,
        grid=(groups, chunks),
        in_specs=[
            rows(inner), rows(heads), rows(heads),
            pl.BlockSpec((1, heads, CHUNK), lambda g, c: (g, 0, c)),
            rows(size), rows(size), whole_block(skip),
            pl.BlockSpec((1, inner, size), lambda g, c: (g, 0, 0)),
        ],
        out_specs=[
            rows(inner),
            pl.BlockSpec((1, 1, inner, size), lambda g, c: (g, c, 0, 0)),
        ],
        out_shape=[
            jax.ShapeDtypeStruct(values.shape, f32),
            jax.ShapeDtypeStruct((groups, chunks, inner, size), bf16),
        ],
        scratch_shapes=[pltpu.VMEM((inner, size), f32)],
        compiler_params=pltpu.CompilerParams(vmem_limit_bytes=40 * 1024 * 1024),
        cost_estimate=pl.CostEstimate(
            flops=20_000_000_000, bytes_accessed=30_000_000, transcendentals=0
        ),
        name="recurrence_forward",
    )(values, steps, cum, cumt, writes, reads, skip, entering)


def run_backward(values, back, core, steps, cum, cumt, writes, reads, skip, states, later, pick):
    groups, length, inner = values.shape
    heads, size = steps.shape[2], writes.shape[2]
    chunks = length // CHUNK

    def rows(width):
        return pl.BlockSpec((1, CHUNK, width), lambda g, c: (g, chunks - 1 - c, 0))

    return pl.pallas_call(
        backward_kernel,
        grid=(groups, chunks),
        in_specs=[
            rows(inner), rows(inner), rows(inner), rows(heads), rows(heads),
            pl.BlockSpec((1, heads, CHUNK), lambda g, c: (g, 0, chunks - 1 - c)),
            rows(size), rows(size), whole_block(skip),
            pl.BlockSpec((1, 1, inner, size), lambda g, c: (g, chunks - 1 - c, 0, 0)),
            pl.BlockSpec((1, inner, size), lambda g, c: (g, 0, 0)),
            whole_block(pick),
        ],
        out_specs=[rows(inner), rows(2 * size), rows(heads), rows(heads)],
        out_shape=[
            jax.ShapeDtypeStruct(values.shape, f32),
            jax.ShapeDtypeStruct((groups, length, 2 * size), f32),
            jax.ShapeDtypeStruct(steps.shape, f32),
            jax.ShapeDtypeStruct(steps.shape, f32),
        ],
        scratch_shapes=[
            pltpu.VMEM((inner, size), f32),
            pltpu.VMEM((inner, size), bf16),
            pltpu.VMEM((CHUNK, inner), bf16),
            pltpu.VMEM((CHUNK, inner), bf16),
            pltpu.VMEM((CHUNK, inner), f32),
            pltpu.VMEM((CHUNK, inner), f32),
        ],
        compiler_params=pltpu.CompilerParams(vmem_limit_bytes=40 * 1024 * 1024),
        cost_estimate=pl.CostEstimate(
            flops=60_000_000_000, bytes_accessed=45_000_000, transcendentals=0
        ),
        name="recurrence_backward",
    )(values, back, core, steps, cum, cumt, writes, reads, skip, states, later, pick)


def from_behind(block, axis, distance):
    devices = range(lax.axis_size(axis))
    route = [(i - distance, i) for i in devices if i - distance in devices]
    return lax.ppermute(block, axis, route)


def reached_state(total, part, axis, reverse, head_width):
    length, index = lax.axis_size(axis), lax.axis_index(axis)
    totals = lax.all_gather(total, axis)
    parts = lax.all_gather(part.astype(bf16), axis)
    result = jnp.zeros(part.shape, f32)
    for k in range(length):
        at = length - 1 - k if reverse else k
        used = at > index if reverse else at < index
        decay = jnp.repeat(jnp.exp(totals[at]), head_width, axis=1)[:, :, None]
        result = jnp.where(used, result * decay + parts[at].astype(f32), result)
    return result


def half_sum(terms):
    if lax.axis_size("head") != 2:
        return lax.psum_scatter(terms, "head", scatter_dimension=1, tiled=True)
    here, half = lax.axis_index("head"), terms.shape[1] // 2
    mine = lax.dynamic_slice_in_dim(terms, here * half, half, 1)
    theirs = lax.dynamic_slice_in_dim(terms, (1 - here) * half, half, 1)
    got = lax.ppermute(theirs.astype(bf16), "head", [(0, 1), (1, 0)])
    return mine + got.astype(f32)


def silu_slope(value):
    logistic = jax.nn.sigmoid(value)
    return logistic * (1.0 + value * (1.0 - logistic))


def convolve(signal, edges, kernel, offset):
    padded = jnp.concatenate([edges, signal], axis=1)
    length = signal.shape[1]
    result = offset + kernel[0] * padded[:, 0:length]
    for position in range(1, kernel.shape[0]):
        result = result + kernel[position] * padded[:, position : position + length]
    return result


def summed_after(part, earlier):
    low = part.astype(bf16)
    if earlier is not None:
        low, earlier = lax.optimization_barrier((low, earlier))
    return lax.psum(low, ("batch", "seq")), earlier


def per_device(
    hidden,
    cotangent,
    norm_gain,
    proj_gate,
    proj_values,
    proj_state,
    proj_steps,
    conv_values,
    conv_state,
    bias_values,
    bias_state,
    step_bias,
    log_rates,
    skip_gain,
    gate_gain,
    proj_output,
):
    groups, length, width_share = hidden.shape
    tokens = groups * length
    whole_rows, gain_whole = (
        lax.all_gather(hidden, "head", axis=2, tiled=True),
        lax.all_gather(norm_gain, "head", axis=0, tiled=True),
    )
    cot_whole = lax.all_gather(cotangent, "head", axis=2, tiled=True).reshape(tokens, -1)
    inputs = whole_rows.astype(f32).reshape(tokens, -1)
    width_full = inputs.shape[1]
    gain_float = gain_whole.astype(f32)
    inv_rms = lax.rsqrt(jnp.mean(inputs * inputs, axis=1, keepdims=True) + epsilon)
    normed = (inputs * inv_rms * gain_float).astype(bf16)
    value_pre = mm(normed, proj_values)
    state_pre = mm(normed, proj_state)
    steps_pre = mm(normed, proj_steps)
    gate_pre = mm(normed, proj_gate)
    inner_share = value_pre.shape[1]
    heads_here = steps_pre.shape[1]
    headdim = inner_share // heads_here
    margin = conv_values.shape[0] - 1

    def conv_in(pre, kernel, offset):
        shaped = pre.reshape(groups, length, -1)
        edges = from_behind(shaped[:, length - margin :], "seq", 1)
        return shaped, edges, convolve(shaped, edges, kernel, offset)

    state_mixed, state_edges, state_conv = conv_in(state_pre, conv_state, bias_state)
    value_mixed, value_edges, value_conv = conv_in(value_pre, conv_values, bias_values)
    values = jax.nn.silu(value_conv)
    maps_full = lax.all_gather(jax.nn.silu(state_conv).astype(bf16), "head", axis=2, tiled=True)
    state_size = maps_full.shape[2] // 2
    writes = maps_full[:, :, :state_size]
    reads = maps_full[:, :, state_size:]
    dt_raw = steps_pre.reshape(groups, length, heads_here)
    steps = jax.nn.softplus(dt_raw + step_bias)
    rates = -jnp.exp(log_rates)
    chunks = length // CHUNK
    lower = jnp.tril(jnp.ones((CHUNK, CHUNK), f32))
    cum4 = jnp.einsum(
        "tu,gcuh->gcth",
        lower,
        (steps * rates).reshape(groups, chunks, CHUNK, heads_here),
        precision=highest,
    )
    cum = cum4.reshape(groups, length, heads_here)
    cumt = jnp.swapaxes(cum, 1, 2)
    ends = cum4[:, :, -1]
    prefix = [jnp.zeros_like(ends[:, 0])]
    for c in range(chunks):
        prefix.append(prefix[-1] + ends[:, c])
    total_log = prefix[-1]
    cumseg = (cum4 + jnp.stack(prefix[:-1], axis=1)[:, :, None]).reshape(cum.shape)

    def lanes(array):
        return jnp.repeat(array, headdim, axis=-1)

    tail = jnp.exp(total_log[:, None] - cumseg) * steps
    zero_final = jnp.einsum(
        "glp,gln->gpn", (values * lanes(tail)).astype(bf16), writes, preferred_element_type=f32
    )
    entering = reached_state(total_log, zero_final, "seq", False, headdim)
    skip = lanes(skip_gain)[None]
    core3, states = run_forward(values, steps, cum, cumt, writes, reads, skip, entering)
    core = core3.reshape(tokens, inner_share)
    gate_act = jax.nn.silu(gate_pre)
    gated = core * gate_act
    square_sum = lax.psum(jnp.sum(gated * gated, axis=1), "head")
    inner_full = inner_share * lax.axis_size("head")
    inv_gate = lax.rsqrt(square_sum / inner_full + epsilon)[:, None]
    gate_unit = gated * inv_gate
    gate_normed = (gate_unit * gate_gain).astype(bf16)
    grad_proj_output = mm(gate_normed, cot_whole, ((0,), (0,)))
    sum_proj_output, _ = summed_after(grad_proj_output, None)
    out_share = half_sum(mm(gate_normed, proj_output))
    block_out = (hidden.astype(f32) + out_share.reshape(hidden.shape)).astype(bf16)
    back_gnorm = mm(cot_whole, proj_output, ((1,), (1,)))
    grad_gate_gain = jnp.sum(back_gnorm * gate_unit, axis=0)
    scaled_gate = back_gnorm * gate_gain
    gate_inner = lax.psum(jnp.sum(scaled_gate * gate_unit, axis=1), "head")
    back_gated = inv_gate * (scaled_gate - gate_unit * (gate_inner / inner_full)[:, None])
    back_core = (back_gated * gate_act).reshape(groups, length, inner_share)
    back_gate = (back_gated * core * silu_slope(gate_pre)).astype(bf16)
    grad_skip_gain = jnp.sum(
        jnp.sum(back_core * values, axis=(0, 1)).reshape(heads_here, headdim), axis=1
    )
    entry_grad = jnp.einsum(
        "glp,gln->gpn",
        (back_core * lanes(jnp.exp(cumseg))).astype(bf16),
        reads,
        preferred_element_type=f32,
    )
    later_grad = reached_state(total_log, entry_grad, "seq", True, headdim)
    grad_proj_gate = mm(normed, back_gate, ((0,), (0,)))
    sum_proj_gate, sum_proj_output = summed_after(grad_proj_gate, sum_proj_output)
    pick = (
        jnp.arange(inner_share)[:, None] // headdim == jnp.arange(heads_here)[None, :]
    ).astype(bf16)
    back_values, back_maps_local, direct, decay_grad = run_backward(
        values, back_core, core3, steps, cum, cumt, writes, reads, skip, states, later_grad, pick
    )
    back_steps = direct + rates * decay_grad
    grad_log_rates = rates * jnp.sum(steps * decay_grad, axis=(0, 1))
    back_dt = back_steps * jax.nn.sigmoid(dt_raw + step_bias)
    grad_step_bias = jnp.sum(back_dt, axis=(0, 1))
    back_maps = half_sum(back_maps_local.reshape(tokens, -1)).reshape(groups, length, -1)

    def conv_out(back_act, conv_pre, mixed, edges, kernel, offset):
        back_conv = back_act * silu_slope(conv_pre)
        padded = jnp.concatenate([edges, mixed], axis=1)
        taps = jnp.stack(
            [
                jnp.sum(back_conv * padded[:, k : k + length], axis=(0, 1))
                for k in range(margin + 1)
            ]
        )
        ahead = from_behind(back_conv[:, :margin], "seq", -1)
        extended = jnp.concatenate([back_conv, ahead], axis=1)
        back = kernel[margin] * back_conv
        for k in range(margin):
            back = back + kernel[k] * extended[:, margin - k : margin - k + length]
        return back.reshape(tokens, -1).astype(bf16), taps, jnp.sum(back_conv, axis=(0, 1))

    back_value_pre, grad_conv_values, grad_bias_values = conv_out(
        back_values, value_conv, value_mixed, value_edges, conv_values, bias_values
    )
    back_state_pre, grad_conv_state, grad_bias_state = conv_out(
        back_maps, state_conv, state_mixed, state_edges, conv_state, bias_state
    )
    back_steps_pre = back_dt.reshape(tokens, heads_here).astype(bf16)
    grad_proj_values = mm(normed, back_value_pre, ((0,), (0,)))
    sum_proj_values, sum_proj_gate = summed_after(grad_proj_values, sum_proj_gate)
    grad_proj_state = mm(normed, back_state_pre, ((0,), (0,)))
    grad_proj_steps = mm(normed, back_steps_pre, ((0,), (0,)))
    across = ((1,), (1,))
    back_normed = mm(back_gate, proj_gate, across) + mm(back_value_pre, proj_values, across)
    back_normed = back_normed + mm(back_state_pre, proj_state, across)
    back_normed = back_normed + mm(back_steps_pre, proj_steps, across)
    normed_total = half_sum(back_normed)
    unit_here = hidden.astype(f32).reshape(tokens, width_share) * inv_rms
    scaled_input = normed_total * norm_gain.astype(f32)
    input_inner = lax.psum(jnp.sum(scaled_input * unit_here, axis=1), "head") / width_full
    back_input = inv_rms * (scaled_input - unit_here * input_inner[:, None])
    grad_norm_gain = jnp.sum(normed_total * unit_here, axis=0)
    grad_hidden = cotangent.astype(f32) + back_input.reshape(hidden.shape)
    small = lax.psum(
        (
            grad_proj_state,
            grad_proj_steps,
            grad_conv_values,
            grad_conv_state,
            grad_bias_values,
            grad_bias_state,
            grad_step_bias,
            grad_log_rates,
            grad_skip_gain,
            grad_gate_gain,
            grad_norm_gain,
        ),
        ("batch", "seq"),
    )
    return (
        block_out,
        grad_hidden,
        small[10],
        sum_proj_gate.astype(f32),
        sum_proj_values.astype(f32),
    ) + small[:10] + (sum_proj_output.astype(f32),)


def solution(mesh):
    in_specs = (
        P("batch", "seq", "head"),
        P("batch", "seq", "head"),
        P("head"),
        P(None, "head"),
        P(None, "head"),
        P(None, "head"),
        P(None, "head"),
        P(None, "head"),
        P(None, "head"),
        P("head"),
        P("head"),
        P("head"),
        P("head"),
        P("head"),
        P("head"),
        P("head", None),
    )
    out_specs = (
        P("batch", "seq", "head"),
        P("batch", "seq", "head"),
        P("head"),
        P(None, "head"),
        P(None, "head"),
        P(None, "head"),
        P(None, "head"),
        P(None, "head"),
        P(None, "head"),
        P("head"),
        P("head"),
        P("head"),
        P("head"),
        P("head"),
        P("head"),
        P("head", None),
    )
    return jax.shard_map(
        per_device, mesh=mesh, in_specs=in_specs, out_specs=out_specs, check_vma=False
    )
```
